1024 devices in a mesh: fsdp: 64 (over z, y_lo), rep: 16 (over x, y_hi, core).
Axes of the slice: x: 4, y: 8 (y_hi: 2, y_lo: 4; y = y_hi * 4 + y_lo), z: 16, core: 2. Of those that a mesh axis runs over, the one named last changes fastest.
Arguments:
- tokens: bfloat16 [7168, 8192], P('rep'), may hold values from -6 to 6
- cotangent: bfloat16 [7168, 16384], P('rep', 'fsdp'), may hold values from -6 to 6
- codes: bfloat16 [8192, 16384], P('rep', 'fsdp'), may hold values from -127 to 127
- scales: bfloat16 [32, 16384], P('rep', 'fsdp'), may hold values from 4.9829483e-05 to 0.00039863586
Outputs:
- activation: bfloat16 [7168, 16384], P(('rep', 'fsdp'))
- weight_grad: float32 [8192, 16384], P('rep', 'fsdp')
The draws below stay inside these ranges and needn't reach their ends.
All inputs are finite; a program needn't handle non-finite values.
Results may differ from the reference program's by a relative error of at most 0.015.
Values may be sent and summed in bfloat16 or wider, within the bound.
A program may use at most 64 MiB of HBM per device.

```python
import math
import jax
import jax.numpy as jnp
from jax import lax

D = 8192
PANEL = 16384
BLOCK_ROWS = 256
TOK_DEV = 448
TOKENS = 7168
N_REP = 16


def raised(values, rng, source, target, parts, factor):
    def block_of(dim):
        return (jnp.arange(values.shape[dim]) // (values.shape[dim] // parts)).reshape((-1,) + (1,) * (values.ndim - 1 - dim))

    first = jax.random.permutation(rng, parts)[block_of(target)]
    second = (block_of(target) + parts // 2) % parts
    return jnp.where((block_of(source) == first) | (block_of(source) == second), factor * values, values)


def level_of(rng, dims, cuts, least, high):
    def one(position, shards_of):
        draws = jax.random.uniform(jax.random.fold_in(jax.random.fold_in(rng, 6), position), (shards_of,), jnp.float32, least / len(cuts), high / len(cuts))
        return jnp.repeat(jnp.exp(draws), dims[position] // shards_of).reshape((-1,) + (1,) * (len(dims) - position - 1))

    level = one(*cuts[0])
    for cut in cuts[1:]:
        level = level * one(*cut)
    return level


def scatter_about(rng, shape, spread, limit, pieces=(), kind=jnp.bfloat16):
    values = jax.random.normal(rng, shape, jnp.float32) * spread
    if len(pieces) > 0:
        values = level_of(rng, shape, pieces, -0.22, 0.18) * values
    return jnp.clip(values, min=-limit, max=limit).astype(kind)


def gaussian_with(key, extent, deviation, most, cuts, heavy, dtype=jnp.bfloat16):
    result = deviation * jax.random.normal(key, extent, jnp.float32)
    if cuts:
        result = result * level_of(key, extent, cuts, -0.22, 0.18)
    return jnp.clip(raised(result, jax.random.fold_in(key, 3), *heavy), -most, most).astype(dtype)


def setup_inputs(seed: int = 0) -> dict:
    key_of = jax.random.split(jax.random.key(seed), 5)
    return {
        "tokens": gaussian_with(key_of[0], (TOKENS, D), 1.0, 6.0, ((0, 16),), (0, 1, 16, 2.0)),
        "cotangent": scatter_about(key_of[1], (TOKENS, PANEL), 1.0, 6.0, ((0, 16), (1, 64))),
        "codes": jnp.clip(jax.random.uniform(key_of[2], (D, PANEL), jnp.float32, -127.0, 127.0) * level_of(key_of[2], (D, PANEL), ((0, 16), (1, 64)), -0.4, 0.0), -127.0, 127.0).astype(jnp.bfloat16),
        "scales": jnp.clip(jnp.exp(math.log(0.00039863586) - 2.0794415 * jax.random.uniform(key_of[3], (D // BLOCK_ROWS, PANEL), jnp.float32) ** level_of(key_of[3], (D // BLOCK_ROWS, PANEL), ((0, 16), (1, 64)), -0.2, 0.2)), 4.982948303222656e-05, 0.00039863586).astype(jnp.bfloat16),
    }


def reference(tokens, cotangent, codes, scales):
    factor = jnp.repeat(scales.astype(jnp.float32), BLOCK_ROWS, axis=0)
    weight = (codes.astype(jnp.float32) * factor).astype(jnp.bfloat16)
    up = jnp.dot(tokens, weight, preferred_element_type=jnp.float32)
    sig = jax.nn.sigmoid(up)
    activation = (up * sig).astype(jnp.bfloat16)
    up_grad = (cotangent.astype(jnp.float32) * sig * (1.0 + up * (1.0 - sig))).astype(jnp.bfloat16)
    token_blocks = tokens.reshape(N_REP, TOK_DEV, D)
    grad_blocks = up_grad.reshape(N_REP, TOK_DEV, PANEL)

    def add_block(total, pair):
        block = jnp.dot(pair[0].T, pair[1], preferred_element_type=jnp.float32).astype(jnp.bfloat16)
        return (total + block.astype(jnp.float32), None)
    total, unused = lax.scan(add_block, jnp.zeros((D, PANEL), jnp.float32), (token_blocks, grad_blocks))
    weight_grad = total / jnp.sqrt(jnp.float32(TOKENS))
    return (activation, weight_grad)
```

```python
import jax
import jax.numpy as jnp
from jax import lax
from jax.experimental import pallas as pl
from jax.experimental.pallas import tpu as pltpu
from jax.sharding import PartitionSpec as P

MESH = pl.DeviceIdType.MESH
BF = jnp.bfloat16
F32 = jnp.float32
NX, NYL, NZ = 4, 4, 16
TOK, D, COLS, ROWS = 448, 8192, 256, 512
HALF = 128
BLOCKS = 8
OWN = 7
INV = 1.0 / (7168.0**0.5)


def body(
    tok, cot, codes, scales, act_o, wg_o,
    T2, CT, CD, W, PS, PR, UGT, AF, S1, S2, A, GK, GS, GR, YS, YR,
    lsem, tsem, trem, wys, wyr, wxs, wxr, pss, psr, gs, gr, gys, gyr, ays, ayr, azs, azr,
):
    f = lax.axis_index("fsdp")
    r = lax.axis_index("rep")
    z, yl = f // NYL, f % NYL
    x, h, c = r // 4, (r // 2) % 2, r % 2

    def rep_of(xx, hh, cc):
        return xx * 4 + hh * 2 + cc

    def at_x(k):
        return (x + k + NX) % NX

    step = (1, -1)
    nbr = [(f, rep_of(at_x(s), h, c)) for s in step]
    anti = (f, rep_of(x, 1 - h, c))
    sib = (f, rep_of(x, h, 1 - c))

    def ylo_peer(j):
        return (z * NYL + (yl + j) % NYL, r)

    def z_peer(i):
        return (((z + i) % NZ) * NYL + yl, r)

    def remote(src, dst, ss, rs, dev):
        return pltpu.make_async_remote_copy(
            src_ref=src, dst_ref=dst, send_sem=ss, recv_sem=rs, device_id=dev, device_id_type=MESH
        )

    sent = []

    def send(cp):
        cp.start()
        sent.append(cp)

    ld_codes = pltpu.make_async_copy(codes, CD, lsem.at[0])
    ld_codes.start()
    barrier = pltpu.get_barrier_semaphore()
    for dev in (nbr[0], nbr[1], anti, sib):
        pl.semaphore_signal(barrier, 1, device_id=dev, device_id_type=MESH)
    for j in range(1, NYL):
        pl.semaphore_signal(barrier, 1, device_id=ylo_peer(j), device_id_type=MESH)

    def greet(i, carry):
        pl.semaphore_signal(barrier, 1, device_id=z_peer(i), device_id_type=MESH)
        return carry

    lax.fori_loop(1, NZ, greet, 0)

    def tok_cols(b, cc):
        return tok.at[:, pl.ds(pl.multiple_of((2 * b + cc) * ROWS, ROWS), ROWS)]

    ld_tok = [pltpu.make_async_copy(tok_cols(b, c), T2.at[c, b], lsem.at[2 + b]) for b in range(BLOCKS)]
    for cp in ld_tok:
        cp.start()
    ld_cot = pltpu.make_async_copy(cot, CT.at[c], lsem.at[1])
    ld_cot.start()

    ld_codes.wait()
    b0 = x * 2 + h
    for p in range(2):
        for k in range(2):
            rows, cols = pl.ds(k * 256, 256), pl.ds(p * HALF, HALF)
            W[b0, p, rows, :] = (
                CD[rows, cols].astype(F32) * scales[pl.ds(k, 1), cols].astype(F32)
            ).astype(BF)

    pl.semaphore_wait(barrier, 4 + (NYL - 1) + (NZ - 1))

    def wpiece(xx, hh, p, q):
        return W.at[xx * 2 + hh, p, pl.ds(q * 256, 256), :]

    def w_y(p, q, mine=True):
        hh = h if mine else 1 - h
        ref = wpiece(x, hh, p, q)
        return remote(ref, ref, wys.at[p, q], wyr.at[p, q], anti)

    def w_x(p, k, d, t, mine=True):
        hh = h if k == 0 else 1 - h
        back = (0 if t < 2 else 1) + (0 if mine else 1)
        q = 1 - d if t == 1 else d
        ref = wpiece(at_x(-step[d] * back), hh, p, q)
        return remote(ref, ref, wxs.at[p, k, d, t], wxr.at[p, k, d, t], nbr[d])

    def w_x_got(p, k, d, t):
        w_x(p, k, d, t, mine=False).wait_recv()

    def forward(p, k):
        for d in range(2):
            w_x_got(p, k, d, 0)
            send(w_x(p, k, d, 2))

    for p in range(2):
        for q in range(2):
            send(w_y(p, q))
        for t in range(2):
            for d in range(2):
                send(w_x(p, 0, d, t))

    tok_out = [remote(tok_cols(b, 1 - c), T2.at[c, b], tsem.at[b], trem.at[b], sib) for b in range(BLOCKS)]
    tok_in = [remote(tok_cols(b, c), T2.at[1 - c, b], tsem.at[b], trem.at[b], sib) for b in range(BLOCKS)]
    for cp in tok_out:
        send(cp)
    send(remote(cot, CT.at[c], tsem.at[8], trem.at[8], sib))
    cot_in = remote(cot, CT.at[1 - c], tsem.at[8], trem.at[8], sib)

    def up_block(xx, hh, p, first=False):
        b = xx * 2 + hh
        w = W[b, p]
        for s in range(2):
            new = jnp.dot(T2[s, b], w, preferred_element_type=F32)
            if first:
                PS[p, s] = new
            else:
                PS[p, s] += new

    def anti_send(p, q):
        w_y(p, q, mine=False).wait_recv()
        send(w_x(p, 1, q, 0))
        send(w_x(p, 1, 1 - q, 1))

    def neighbours(p, k):
        hh = h if k == 0 else 1 - h
        for d in range(2):
            w_x_got(p, k, d, 1)
        for d in range(2):
            up_block(at_x(-step[d]), hh, p)

    def far(p, k):
        hh = h if k == 0 else 1 - h
        for d in range(2):
            w_x_got(p, k, d, 2)
        up_block(at_x(2), hh, p)

    partial = [remote(PS.at[p], PR.at[p], pss.at[p], psr.at[p], sib) for p in range(2)]

    forward(0, 0)
    forward(1, 0)
    anti_send(0, 0)
    for cp in ld_tok:
        cp.wait()
    for cp in tok_in:
        cp.wait_recv()
    for p in range(2):
        up_block(x, h, p, first=True)
    anti_send(0, 1)
    neighbours(0, 0)
    far(0, 0)
    up_block(x, 1 - h, 0)
    anti_send(1, 0)
    neighbours(1, 0)
    forward(0, 1)
    far(1, 0)
    anti_send(1, 1)
    up_block(x, 1 - h, 1)
    neighbours(0, 1)
    far(0, 1)
    send(partial[0])
    forward(1, 1)
    ld_cot.wait()
    cot_in.wait_recv()

    def gradient(p):
        partial[p].wait_recv()
        for s in range(2):
            up = PS[p, s] + PR[p, s]
            sig = jax.nn.sigmoid(up)
            g = CT[s, :, pl.ds(p * HALF, HALF)].astype(F32) * sig * (1.0 + up * (1.0 - sig))
            UGT[p, s] = g.T.astype(BF)

    def act_y(p, j, mine=True):
        to = (yl + j) % NYL
        frm = yl if mine else (yl - j + NYL) % NYL
        return remote(S1.at[p, to], S2.at[p, frm], ays.at[p, j], ayr.at[p, j], ylo_peer(j))

    def act_z(p, i, mine=True):
        to = (z + i) % NZ
        frm = z if mine else (z - i + NZ) % NZ
        return remote(S2.at[p, :, to], A.at[p, frm], azs.at[p, i], azr.at[p, i], z_peer(i))

    def activation_out(p):
        up = PS[p, c] + PR[p, c]
        AF[p, pl.ds(0, TOK), :] = up * jax.nn.sigmoid(up)
        AF[p, pl.ds(TOK, 8), :] = jnp.zeros((8, HALF), F32)
        for to in range(NYL):
            for zz in range(NZ):
                S1[p, to, zz] = AF[p, pl.ds(OWN * (zz * NYL + to), 8), :].astype(BF)
        for j in range(1, NYL):
            send(act_y(p, j))
        S2[p, yl] = S1[p, yl]

    def activation_z(p):
        for j in range(1, NYL):
            act_y(p, j, mine=False).wait_recv()

        def go(i, carry):
            act_z(p, i).start()
            return carry

        lax.fori_loop(1, NZ, go, 0)
        A[p, z] = S2[p, :, z]

    def activation_end(p):
        def got(i, carry):
            act_z(p, i, mine=False).wait_recv()
            return carry

        lax.fori_loop(1, NZ, got, 0)
        for zz in range(NZ):
            for y4 in range(NYL):
                col = (zz * NYL + y4) * COLS + p * HALF
                act_o[:, pl.ds(col, HALF)] = A[p, zz, y4][:OWN, :]

    def grad_block(p, xx, hh):
        b = xx * 2 + hh
        return jnp.dot(UGT[p, 0], T2[0, b], preferred_element_type=F32) + jnp.dot(
            UGT[p, 1], T2[1, b], preferred_element_type=F32
        )

    def g_x(p, k, d, t):
        return remote(GS.at[p, k, d, t], GR.at[p, k, d, t], gs.at[p, k, d, t], gr.at[p, k, d, t], nbr[d])

    def halves(v, q):
        return v[q * 64 : (q + 1) * 64, :]

    def scatter_first(p, k):
        hh = 1 - h if k == 0 else h
        g = grad_block(p, at_x(2), hh)
        for d in range(2):
            GS[p, k, d, 0] = halves(g, d).astype(BF)
            send(g_x(p, k, d, 0))
        for d in range(2):
            g = grad_block(p, at_x(step[d]), hh)
            GS[p, k, d, 1] = halves(g, 1 - d).astype(BF)
            send(g_x(p, k, d, 1))
            GK[p, k, d] = halves(g, d)
        g = grad_block(p, x, hh)
        for q in range(2):
            GK[p, k, 2 + q] = halves(g, q)

    def scatter_second(p, k):
        for d in range(2):
            g_x(p, k, d, 0).wait_recv()
            GS[p, k, d, 2] = (GK[p, k, d] + GR[p, k, d, 0].astype(F32)).astype(BF)
            send(g_x(p, k, d, 2))

    def scatter_sum(p, k, q):
        return GK[p, k, 2 + q] + GR[p, k, 1 - q, 1].astype(F32) + GR[p, k, q, 2].astype(F32)

    def scatter_got(p, k):
        for d in range(2):
            g_x(p, k, d, 1).wait_recv()
        for d in range(2):
            g_x(p, k, d, 2).wait_recv()

    g_y = [remote(YS.at[p], YR.at[p], gys.at[p], gyr.at[p], anti) for p in range(2)]

    def cross(p):
        scatter_got(p, 0)
        for q in range(2):
            YS[p, pl.ds(q * 64, 64), :] = scatter_sum(p, 0, q).astype(BF)
        send(g_y[p])

    def finish(p):
        scatter_got(p, 1)
        g_y[p].wait_recv()
        total = jnp.concatenate(
            [scatter_sum(p, 1, q) + YR[p, pl.ds(q * 64, 64), :].astype(F32) for q in range(2)], axis=0
        )
        wg_o[:, pl.ds(p * HALF, HALF)] = total.T * INV

    gradient(0)
    scatter_first(0, 0)
    activation_out(0)
    neighbours(1, 1)
    far(1, 1)
    send(partial[1])
    scatter_second(0, 0)
    gradient(1)
    scatter_first(1, 0)
    activation_out(1)
    scatter_first(0, 1)
    activation_z(0)
    cross(0)
    scatter_second(1, 0)
    scatter_first(1, 1)
    activation_z(1)
    scatter_second(0, 1)
    cross(1)
    scatter_second(1, 1)
    activation_end(0)
    finish(0)
    activation_end(1)
    finish(1)

    for cp in sent:
        cp.wait_send()

    def done(i, carry):
        for p in range(2):
            act_z(p, i).wait_send()
        return carry

    lax.fori_loop(1, NZ, done, 0)


def per_device(tokens, cotangent, codes, scales):
    dma = pltpu.SemaphoreType.DMA
    hbm = pl.BlockSpec(memory_space=pl.ANY)
    vmem = pl.BlockSpec(memory_space=pltpu.VMEM)
    return pl.pallas_call(
        body,
        out_shape=(
            jax.ShapeDtypeStruct((OWN, NZ * NYL * COLS), BF),
            jax.ShapeDtypeStruct((ROWS, COLS), F32),
        ),
        in_specs=[hbm, hbm, hbm, vmem],
        out_specs=(vmem, vmem),
        scratch_shapes=[
            pltpu.VMEM((2, BLOCKS, TOK, ROWS), BF),
            pltpu.VMEM((2, TOK, COLS), BF),
            pltpu.VMEM((ROWS, COLS), BF),
            pltpu.VMEM((BLOCKS, 2, ROWS, HALF), BF),
            pltpu.VMEM((2, 2, TOK, HALF), F32),
            pltpu.VMEM((2, 2, TOK, HALF), F32),
            pltpu.VMEM((2, 2, HALF, TOK), BF),
            pltpu.VMEM((2, TOK + 8, HALF), F32),
            pltpu.VMEM((2, NYL, NZ, 8, HALF), BF),
            pltpu.VMEM((2, NYL, NZ, 8, HALF), BF),
            pltpu.VMEM((2, NZ, NYL, 8, HALF), BF),
            pltpu.VMEM((2, 2, 4, 64, ROWS), F32),
            pltpu.VMEM((2, 2, 2, 3, 64, ROWS), BF),
            pltpu.VMEM((2, 2, 2, 3, 64, ROWS), BF),
            pltpu.VMEM((2, HALF, ROWS), BF),
            pltpu.VMEM((2, HALF, ROWS), BF),
            dma((2 + BLOCKS,)),
            dma((9,)), dma((9,)),
            dma((2, 2)), dma((2, 2)),
            dma((2, 2, 2, 3)), dma((2, 2, 2, 3)),
            dma((2,)), dma((2,)),
            dma((2, 2, 2, 3)), dma((2, 2, 2, 3)),
            dma((2,)), dma((2,)),
            dma((2, NYL)), dma((2, NYL)),
            dma((2, NZ)), dma((2, NZ)),
        ],
        compiler_params=pltpu.CompilerParams(
            collective_id=0, has_side_effects=True, vmem_limit_bytes=48 << 20
        ),
        name="panel",
    )(tokens, cotangent, codes, scales)


def solution(mesh):
    return jax.shard_map(
        per_device,
        mesh=mesh,
        in_specs=(P("rep", None), P("rep", "fsdp"), P("rep", "fsdp"), P("rep", "fsdp")),
        out_specs=(P(("rep", "fsdp"), None), P("rep", "fsdp")),
        check_vma=False,
    )
```

```python
import jax
import jax.numpy as jnp
from jax import lax
from jax.experimental import pallas as pl
from jax.experimental.pallas import tpu as pltpu
from jax.sharding import PartitionSpec as P

MESH = pl.DeviceIdType.MESH
BF = jnp.bfloat16
F32 = jnp.float32
NX, NYL, NZ = 4, 4, 16
TOK, D, COLS, ROWS = 448, 8192, 256, 512
HALF = 128
BLOCKS = 8
OWN = 7
INV = 1.0 / (7168.0**0.5)


def body(
    tok, cot, codes, scales, act_o, wg_o,
    T2, CT, CD, SC, W, PS, PR, UGT, AF, S1, S2, A, GK, GS, GR, YS, YR,
    lsem, tsem, trem, wys, wyr, wxs, wxr, pss, psr, gs, gr, gys, gyr, ays, ayr, azs, azr, zin,
):
    f = lax.axis_index("fsdp")
    r = lax.axis_index("rep")
    z, yl = f // NYL, f % NYL
    x, h, c = r // 4, (r // 2) % 2, r % 2

    def rep_of(xx, hh, cc):
        return xx * 4 + hh * 2 + cc

    def at_x(k):
        return (x + k + NX) % NX

    step = (1, -1)
    nbr = [(f, rep_of(at_x(s), h, c)) for s in step]
    anti = (f, rep_of(x, 1 - h, c))
    sib = (f, rep_of(x, h, 1 - c))

    def ylo_peer(j):
        return (z * NYL + (yl + j) % NYL, r)

    def z_peer(i):
        return (((z + i) % NZ) * NYL + yl, r)

    def remote(src, dst, ss, rs, dev):
        return pltpu.make_async_remote_copy(
            src_ref=src, dst_ref=dst, send_sem=ss, recv_sem=rs, device_id=dev, device_id_type=MESH
        )

    sent = []

    def send(cp):
        cp.start()
        sent.append(cp)

    ld_codes = pltpu.make_async_copy(codes, CD, lsem.at[0])
    ld_codes.start()
    ld_scales = pltpu.make_async_copy(scales, SC, lsem.at[2])
    ld_scales.start()
    barrier = pltpu.get_barrier_semaphore()
    for dev in (nbr[0], nbr[1], anti, sib):
        pl.semaphore_signal(barrier, 1, device_id=dev, device_id_type=MESH)
    for j in range(1, NYL):
        pl.semaphore_signal(barrier, 1, device_id=ylo_peer(j), device_id_type=MESH)

    def z_say(sem, k):
        for s in (k, -k):
            @pl.when((z + s >= 0) & (z + s < NZ))
            def _():
                pl.semaphore_signal(sem, 1, device_id=((z + s) * NYL + yl, r), device_id_type=MESH)

    def z_count(k):
        return jnp.where(z >= k, 1, 0) + jnp.where(z + k < NZ, 1, 0)

    z_say(barrier, 1)

    def z_round(k):
        if k > 0:
            pl.semaphore_wait(zin.at[k - 1], z_count(1 << (k - 1)))
        if k < 4:
            z_say(zin.at[k], 1 << k)

    def tok_cols(b, cc):
        return tok.at[:, pl.ds(pl.multiple_of((2 * b + cc) * ROWS, ROWS), ROWS)]

    ld_tok = [pltpu.make_async_copy(tok_cols(b, c), T2.at[c, b], lsem.at[3 + b]) for b in range(BLOCKS)]
    for cp in ld_tok:
        cp.start()
    ld_cot = pltpu.make_async_copy(cot, CT.at[c], lsem.at[1])
    ld_cot.start()

    ld_codes.wait()
    ld_scales.wait()
    b0 = x * 2 + h
    for p in range(2):
        for k in range(2):
            rows, cols = pl.ds(k * 256, 256), pl.ds(p * HALF, HALF)
            W[b0, p, rows, :] = (
                CD[rows, cols].astype(F32) * SC[pl.ds(k, 1), cols].astype(F32)
            ).astype(BF)

    pl.semaphore_wait(barrier, 4 + (NYL - 1) + z_count(1))

    def wpiece(xx, hh, p, q):
        return W.at[xx * 2 + hh, p, pl.ds(q * 256, 256), :]

    def w_y(p, q, mine=True):
        hh = h if mine else 1 - h
        ref = wpiece(x, hh, p, q)
        return remote(ref, ref, wys.at[p, q], wyr.at[p, q], anti)

    def w_x(p, k, d, t, mine=True):
        hh = h if k == 0 else 1 - h
        back = (0 if t < 2 else 1) + (0 if mine else 1)
        q = 1 - d if t == 1 else d
        ref = wpiece(at_x(-step[d] * back), hh, p, q)
        return remote(ref, ref, wxs.at[p, k, d, t], wxr.at[p, k, d, t], nbr[d])

    def w_x_got(p, k, d, t):
        w_x(p, k, d, t, mine=False).wait_recv()

    def forward(p, k):
        for d in range(2):
            w_x_got(p, k, d, 0)
            send(w_x(p, k, d, 2))

    for p in range(2):
        for q in range(2):
            send(w_y(p, q))
        for t in range(2):
            for d in range(2):
                send(w_x(p, 0, d, t))

    tok_out = [remote(tok_cols(b, 1 - c), T2.at[c, b], tsem.at[b], trem.at[b], sib) for b in range(BLOCKS)]
    tok_in = [remote(tok_cols(b, c), T2.at[1 - c, b], tsem.at[b], trem.at[b], sib) for b in range(BLOCKS)]
    for cp in tok_out:
        send(cp)
    send(remote(cot, CT.at[c], tsem.at[8], trem.at[8], sib))
    cot_in = remote(cot, CT.at[1 - c], tsem.at[8], trem.at[8], sib)

    def up_block(xx, hh, p, first=False):
        b = xx * 2 + hh
        w = W[b, p]
        for s in range(2):
            new = jnp.dot(T2[s, b], w, preferred_element_type=F32)
            if first:
                PS[p, s] = new
            else:
                PS[p, s] += new

    def anti_send(p, q):
        w_y(p, q, mine=False).wait_recv()
        send(w_x(p, 1, q, 0))
        send(w_x(p, 1, 1 - q, 1))

    def neighbours(p, k):
        hh = h if k == 0 else 1 - h
        for d in range(2):
            w_x_got(p, k, d, 1)
        for d in range(2):
            up_block(at_x(-step[d]), hh, p)

    def far(p, k):
        hh = h if k == 0 else 1 - h
        for d in range(2):
            w_x_got(p, k, d, 2)
        up_block(at_x(2), hh, p)

    partial = [remote(PS.at[p], PR.at[p], pss.at[p], psr.at[p], sib) for p in range(2)]

    z_round(0)
    forward(0, 0)
    forward(1, 0)
    anti_send(0, 0)
    z_round(1)
    for cp in ld_tok:
        cp.wait()
    for cp in tok_in:
        cp.wait_recv()
    up_block(x, h, 0, first=True)
    anti_send(0, 1)
    z_round(2)
    up_block(x, h, 1, first=True)
    neighbours(0, 0)
    far(0, 0)
    anti_send(1, 0)
    up_block(x, 1 - h, 0)
    forward(0, 1)
    neighbours(1, 0)
    anti_send(1, 1)
    z_round(3)
    far(1, 0)
    up_block(x, 1 - h, 1)
    neighbours(0, 1)
    forward(1, 1)
    far(0, 1)
    send(partial[0])
    ld_cot.wait()
    cot_in.wait_recv()

    def gradient(p):
        for s in range(2):
            up = PS[p, s] + PR[p, s]
            sig = jax.nn.sigmoid(up)
            g = CT[s, :, pl.ds(p * HALF, HALF)].astype(F32) * sig * (1.0 + up * (1.0 - sig))
            UGT[p, s] = g.T.astype(BF)

    def act_y(p, j, mine=True):
        to = (yl + j) % NYL
        frm = yl if mine else (yl - j + NYL) % NYL
        return remote(S1.at[p, to], S2.at[p, frm], ays.at[p, j], ayr.at[p, j], ylo_peer(j))

    def act_z(p, i, mine=True):
        to = (z + i) % NZ
        frm = z if mine else (z - i + NZ) % NZ
        return remote(S2.at[p, :, to], A.at[p, frm], azs.at[p, i], azr.at[p, i], z_peer(i))

    def activation_out(p):
        up = PS[p, c] + PR[p, c]
        AF[p, pl.ds(0, TOK), :] = up * jax.nn.sigmoid(up)
        AF[p, pl.ds(TOK, 8), :] = jnp.zeros((8, HALF), F32)
        for to in range(NYL):
            for zz in range(NZ):
                S1[p, to, zz] = AF[p, pl.ds(OWN * (zz * NYL + to), 8), :].astype(BF)
        for j in range(1, NYL):
            send(act_y(p, j))
        S2[p, yl] = S1[p, yl]

    def activation_z(p):
        for j in range(1, NYL):
            act_y(p, j, mine=False).wait_recv()

        def go(i, carry):
            act_z(p, i).start()
            return carry

        lax.fori_loop(1, NZ, go, 0)
        A[p, z] = S2[p, :, z]

    def activation_end(p):
        def got(i, carry):
            act_z(p, i, mine=False).wait_recv()
            return carry

        lax.fori_loop(1, NZ, got, 0)
        for zz in range(NZ):
            for y4 in range(NYL):
                col = (zz * NYL + y4) * COLS + p * HALF
                act_o[:, pl.ds(col, HALF)] = A[p, zz, y4][:OWN, :]

    def grad_block(p, xx, hh):
        b = xx * 2 + hh
        return jnp.dot(UGT[p, 0], T2[0, b], preferred_element_type=F32) + jnp.dot(
            UGT[p, 1], T2[1, b], preferred_element_type=F32
        )

    def g_x(p, k, d, t):
        return remote(GS.at[p, k, d, t], GR.at[p, k, d, t], gs.at[p, k, d, t], gr.at[p, k, d, t], nbr[d])

    def halves(v, q):
        return v[q * 64 : (q + 1) * 64, :]

    def scatter_first(p, k):
        hh = 1 - h if k == 0 else h
        g = grad_block(p, at_x(2), hh)
        for d in range(2):
            GS[p, k, d, 0] = halves(g, d).astype(BF)
            send(g_x(p, k, d, 0))
        for d in range(2):
            g = grad_block(p, at_x(step[d]), hh)
            GS[p, k, d, 1] = halves(g, 1 - d).astype(BF)
            send(g_x(p, k, d, 1))
            GK[p, k, d] = halves(g, d)
        g = grad_block(p, x, hh)
        for q in range(2):
            GK[p, k, 2 + q] = halves(g, q)

    def scatter_second(p, k):
        for d in range(2):
            g_x(p, k, d, 0).wait_recv()
            GS[p, k, d, 2] = (GK[p, k, d] + GR[p, k, d, 0].astype(F32)).astype(BF)
            send(g_x(p, k, d, 2))

    def scatter_sum(p, k, q):
        return GK[p, k, 2 + q] + GR[p, k, 1 - q, 1].astype(F32) + GR[p, k, q, 2].astype(F32)

    def scatter_got(p, k):
        for d in range(2):
            g_x(p, k, d, 1).wait_recv()
        for d in range(2):
            g_x(p, k, d, 2).wait_recv()

    g_y = [remote(YS.at[p], YR.at[p], gys.at[p], gyr.at[p], anti) for p in range(2)]

    def cross(p):
        scatter_got(p, 0)
        for q in range(2):
            YS[p, pl.ds(q * 64, 64), :] = scatter_sum(p, 0, q).astype(BF)
        send(g_y[p])

    def finish(p):
        scatter_got(p, 1)
        g_y[p].wait_recv()
        total = jnp.concatenate(
            [scatter_sum(p, 1, q) + YR[p, pl.ds(q * 64, 64), :].astype(F32) for q in range(2)], axis=0
        )
        wg_o[:, pl.ds(p * HALF, HALF)] = total.T * INV

    partial[0].wait_recv()
    activation_out(0)
    gradient(0)
    neighbours(1, 1)
    far(1, 1)
    send(partial[1])
    scatter_first(0, 0)
    z_round(4)
    activation_z(0)
    partial[1].wait_recv()
    activation_out(1)
    gradient(1)
    scatter_second(0, 0)
    scatter_first(1, 0)
    activation_z(1)
    scatter_first(0, 1)
    cross(0)
    scatter_second(1, 0)
    scatter_first(1, 1)
    scatter_second(0, 1)
    cross(1)
    scatter_second(1, 1)
    finish(0)
    activation_end(0)
    finish(1)
    activation_end(1)

    for cp in sent:
        cp.wait_send()

    def done(i, carry):
        for p in range(2):
            act_z(p, i).wait_send()
        return carry

    lax.fori_loop(1, NZ, done, 0)


def hand_over(act, wg, act_o, wg_o, act_v, wg_v, sem):
    into = [
        pltpu.make_async_copy(wg, wg_v, sem.at[0]),
        pltpu.make_async_copy(act, act_v, sem.at[1]),
    ]
    out = [
        pltpu.make_async_copy(wg_v, wg_o, sem.at[2]),
        pltpu.make_async_copy(act_v, act_o, sem.at[3]),
    ]
    for cp in into:
        cp.start()
    for arrived, cp in zip(into, out):
        arrived.wait()
        cp.start()
    for cp in out:
        cp.wait()


def per_device(tokens, cotangent, codes, scales):
    dma = pltpu.SemaphoreType.DMA
    hbm = pl.BlockSpec(memory_space=pltpu.HBM)
    vmem = pl.BlockSpec(memory_space=pltpu.VMEM)
    out_shape = (
        jax.ShapeDtypeStruct((OWN, NZ * NYL * COLS), BF),
        jax.ShapeDtypeStruct((ROWS, COLS), F32),
    )
    act, wg = pl.pallas_call(
        body,
        out_shape=out_shape,
        in_specs=[hbm, hbm, hbm, hbm],
        out_specs=(vmem, vmem),
        scratch_shapes=[
            pltpu.VMEM((2, BLOCKS, TOK, ROWS), BF),
            pltpu.VMEM((2, TOK, COLS), BF),
            pltpu.VMEM((ROWS, COLS), BF),
            pltpu.VMEM((2, COLS), BF),
            pltpu.VMEM((BLOCKS, 2, ROWS, HALF), BF),
            pltpu.VMEM((2, 2, TOK, HALF), F32),
            pltpu.VMEM((2, 2, TOK, HALF), F32),
            pltpu.VMEM((2, 2, HALF, TOK), BF),
            pltpu.VMEM((2, TOK + 8, HALF), F32),
            pltpu.VMEM((2, NYL, NZ, 8, HALF), BF),
            pltpu.VMEM((2, NYL, NZ, 8, HALF), BF),
            pltpu.VMEM((2, NZ, NYL, 8, HALF), BF),
            pltpu.VMEM((2, 2, 4, 64, ROWS), F32),
            pltpu.VMEM((2, 2, 2, 3, 64, ROWS), BF),
            pltpu.VMEM((2, 2, 2, 3, 64, ROWS), BF),
            pltpu.VMEM((2, HALF, ROWS), BF),
            pltpu.VMEM((2, HALF, ROWS), BF),
            dma((3 + BLOCKS,)),
            dma((9,)), dma((9,)),
            dma((2, 2)), dma((2, 2)),
            dma((2, 2, 2, 3)), dma((2, 2, 2, 3)),
            dma((2,)), dma((2,)),
            dma((2, 2, 2, 3)), dma((2, 2, 2, 3)),
            dma((2,)), dma((2,)),
            dma((2, NYL)), dma((2, NYL)),
            dma((2, NZ)), dma((2, NZ)),
            pltpu.SemaphoreType.REGULAR((4,)),
        ],
        compiler_params=pltpu.CompilerParams(
            collective_id=0, has_side_effects=True, vmem_limit_bytes=61 << 20
        ),
        name="panel",
    )(tokens, cotangent, codes, scales)
    return pl.pallas_call(
        hand_over,
        out_shape=out_shape,
        in_specs=[hbm, hbm],
        out_specs=(hbm, hbm),
        scratch_shapes=[
            pltpu.VMEM((OWN, NZ * NYL * COLS), BF),
            pltpu.VMEM((ROWS, COLS), F32),
            dma((4,)),
        ],
        compiler_params=pltpu.CompilerParams(vmem_limit_bytes=61 << 20),
        name="hand_over",
    )(act, wg)


def solution(mesh):
    return jax.shard_map(
        per_device,
        mesh=mesh,
        in_specs=(P("rep", None), P("rep", "fsdp"), P("rep", "fsdp"), P("rep", "fsdp")),
        out_specs=(P(("rep", "fsdp"), None), P("rep", "fsdp")),
        check_vma=False,
    )
```

```python
import jax
import jax.numpy as jnp
from jax import lax
from jax.experimental import pallas as pl
from jax.experimental.pallas import tpu as pltpu
from jax.sharding import PartitionSpec as P

MESH = pl.DeviceIdType.MESH
BF = jnp.bfloat16
F32 = jnp.float32
NX, NYL, NZ = 4, 4, 16
TOK, D, COLS, ROWS = 448, 8192, 256, 512
HALF = 128
BLOCKS = 8
OWN = 7
INV = 1.0 / (7168.0**0.5)


def body(
    tok, cot, codes, scales, act_o, wg_o,
    T2, CT, CD, SC, W, PS, PR, UGT, AF, S1, S2, A, GK, GS, GR, YS, YR,
    lsem, tsem, trem, wys, wyr, wxs, wxr, pss, psr, gs, gr, gys, gyr, ays, ayr, azs, azr, zin,
):
    f = lax.axis_index("fsdp")
    r = lax.axis_index("rep")
    z, yl = f // NYL, f % NYL
    x, h, c = r // 4, (r // 2) % 2, r % 2

    def rep_of(xx, hh, cc):
        return xx * 4 + hh * 2 + cc

    def at_x(k):
        return (x + k + NX) % NX

    step = (1, -1)
    nbr = [(f, rep_of(at_x(s), h, c)) for s in step]
    anti = (f, rep_of(x, 1 - h, c))
    sib = (f, rep_of(x, h, 1 - c))

    def ylo_peer(j):
        return (z * NYL + (yl + j) % NYL, r)

    def z_peer(i):
        return (((z + i) % NZ) * NYL + yl, r)

    def remote(src, dst, ss, rs, dev):
        return pltpu.make_async_remote_copy(
            src_ref=src, dst_ref=dst, send_sem=ss, recv_sem=rs, device_id=dev, device_id_type=MESH
        )

    sent = []

    def send(cp):
        cp.start()
        sent.append(cp)

    ld_codes = pltpu.make_async_copy(codes, CD, lsem.at[0])
    ld_codes.start()
    ld_scales = pltpu.make_async_copy(scales, SC, lsem.at[2])
    ld_scales.start()
    barrier = pltpu.get_barrier_semaphore()
    for dev in (nbr[0], nbr[1], anti, sib):
        pl.semaphore_signal(barrier, 1, device_id=dev, device_id_type=MESH)
    for j in range(1, NYL):
        pl.semaphore_signal(barrier, 1, device_id=ylo_peer(j), device_id_type=MESH)

    def z_say(sem, k):
        for s in (k, -k):
            @pl.when((z + s >= 0) & (z + s < NZ))
            def _():
                pl.semaphore_signal(sem, 1, device_id=((z + s) * NYL + yl, r), device_id_type=MESH)

    def z_count(k):
        return jnp.where(z >= k, 1, 0) + jnp.where(z + k < NZ, 1, 0)

    z_say(barrier, 1)

    def z_round(k):
        if k > 0:
            pl.semaphore_wait(zin.at[k - 1], z_count(1 << (k - 1)))
        if k < 4:
            z_say(zin.at[k], 1 << k)

    def tok_cols(b, cc):
        return tok.at[:, pl.ds(pl.multiple_of((2 * b + cc) * ROWS, ROWS), ROWS)]

    ld_tok = [pltpu.make_async_copy(tok_cols(b, c), T2.at[c, b], lsem.at[3 + b]) for b in range(BLOCKS)]
    for cp in ld_tok:
        cp.start()
    ld_cot = pltpu.make_async_copy(cot, CT.at[c], lsem.at[1])
    ld_cot.start()

    ld_codes.wait()
    ld_scales.wait()
    b0 = x * 2 + h
    for p in range(2):
        for k in range(2):
            rows, cols = pl.ds(k * 256, 256), pl.ds(p * HALF, HALF)
            W[b0, p, rows, :] = (
                CD[rows, cols].astype(F32) * SC[pl.ds(k, 1), cols].astype(F32)
            ).astype(BF)

    pl.semaphore_wait(barrier, 4 + (NYL - 1) + z_count(1))

    def wpiece(xx, hh, p, q):
        return W.at[xx * 2 + hh, p, pl.ds(q * 256, 256), :]

    def w_y(p, q, mine=True):
        hh = h if mine else 1 - h
        ref = wpiece(x, hh, p, q)
        return remote(ref, ref, wys.at[p, q], wyr.at[p, q], anti)

    def w_x(p, k, d, t, mine=True):
        hh = h if k == 0 else 1 - h
        back = (0 if t < 2 else 1) + (0 if mine else 1)
        q = 1 - d if t == 1 else d
        ref = wpiece(at_x(-step[d] * back), hh, p, q)
        return remote(ref, ref, wxs.at[p, k, d, t], wxr.at[p, k, d, t], nbr[d])

    def w_x_got(p, k, d, t):
        w_x(p, k, d, t, mine=False).wait_recv()

    def forward(p, k):
        for d in range(2):
            w_x_got(p, k, d, 0)
            send(w_x(p, k, d, 2))

    for p in range(2):
        for q in range(2):
            send(w_y(p, q))
        for t in range(2):
            for d in range(2):
                send(w_x(p, 0, d, t))

    tok_out = [remote(tok_cols(b, 1 - c), T2.at[c, b], tsem.at[b], trem.at[b], sib) for b in range(BLOCKS)]
    tok_in = [remote(tok_cols(b, c), T2.at[1 - c, b], tsem.at[b], trem.at[b], sib) for b in range(BLOCKS)]
    for cp in tok_out:
        send(cp)
    send(remote(cot, CT.at[c], tsem.at[8], trem.at[8], sib))
    cot_in = remote(cot, CT.at[1 - c], tsem.at[8], trem.at[8], sib)

    def up_block(xx, hh, p, first=False):
        b = xx * 2 + hh
        w = W[b, p]
        for s in range(2):
            new = jnp.dot(T2[s, b], w, preferred_element_type=F32)
            if first:
                PS[p, s] = new
            else:
                PS[p, s] += new

    def anti_send(p, q):
        w_y(p, q, mine=False).wait_recv()
        send(w_x(p, 1, q, 0))
        send(w_x(p, 1, 1 - q, 1))

    def neighbours(p, k):
        hh = h if k == 0 else 1 - h
        for d in range(2):
            w_x_got(p, k, d, 1)
        for d in range(2):
            up_block(at_x(-step[d]), hh, p)

    def far(p, k):
        hh = h if k == 0 else 1 - h
        for d in range(2):
            w_x_got(p, k, d, 2)
        up_block(at_x(2), hh, p)

    partial = [remote(PS.at[p], PR.at[p], pss.at[p], psr.at[p], sib) for p in range(2)]

    z_round(0)
    forward(0, 0)
    forward(1, 0)
    anti_send(0, 0)
    z_round(1)
    for cp in ld_tok:
        cp.wait()
    for cp in tok_in:
        cp.wait_recv()
    up_block(x, h, 0, first=True)
    anti_send(0, 1)
    z_round(2)
    up_block(x, h, 1, first=True)
    neighbours(0, 0)
    far(0, 0)
    anti_send(1, 0)
    up_block(x, 1 - h, 0)
    forward(0, 1)
    neighbours(1, 0)
    anti_send(1, 1)
    z_round(3)
    far(1, 0)
    up_block(x, 1 - h, 1)
    neighbours(0, 1)
    forward(1, 1)
    far(0, 1)
    send(partial[0])
    ld_cot.wait()
    cot_in.wait_recv()

    def gradient(p):
        for s in range(2):
            up = PS[p, s] + PR[p, s]
            sig = jax.nn.sigmoid(up)
            g = CT[s, :, pl.ds(p * HALF, HALF)].astype(F32) * sig * (1.0 + up * (1.0 - sig))
            UGT[p, s] = g.T.astype(BF)

    def act_y(p, j, mine=True):
        to = (yl + j) % NYL
        frm = yl if mine else (yl - j + NYL) % NYL
        return remote(S1.at[p, to], S2.at[p, frm], ays.at[p, j], ayr.at[p, j], ylo_peer(j))

    def act_z(p, i):
        to = (z + i) % NZ
        return remote(S2.at[p, :, to], A.at[p, z], azs.at[p], azr.at[p], z_peer(i))

    def act_z_all(p):
        part = A.at[p, pl.ds(0, NZ - 1)]
        return remote(part, part, azs.at[p], azr.at[p], sib)

    def activation_out(p):
        up = PS[p, c] + PR[p, c]
        AF[p, pl.ds(0, TOK), :] = up * jax.nn.sigmoid(up)
        AF[p, pl.ds(TOK, 8), :] = jnp.zeros((8, HALF), F32)
        for to in range(NYL):
            for zz in range(NZ):
                S1[p, to, zz] = AF[p, pl.ds(OWN * (zz * NYL + to), 8), :].astype(BF)
        for j in range(1, NYL):
            send(act_y(p, j))
        S2[p, yl] = S1[p, yl]

    def activation_z(p):
        for j in range(1, NYL):
            act_y(p, j, mine=False).wait_recv()

        def go(i, carry):
            act_z(p, i).start()
            return carry

        lax.fori_loop(1, NZ, go, 0)
        A[p, z] = S2[p, :, z]

    def activation_end(p):
        act_z_all(p).wait_recv()
        for zz in range(NZ):
            for y4 in range(NYL):
                col = (zz * NYL + y4) * COLS + p * HALF
                act_o[:, pl.ds(col, HALF)] = A[p, zz, y4][:OWN, :]

    def grad_block(p, xx, hh):
        b = xx * 2 + hh
        return jnp.dot(UGT[p, 0], T2[0, b], preferred_element_type=F32) + jnp.dot(
            UGT[p, 1], T2[1, b], preferred_element_type=F32
        )

    def g_x(p, k, d, t):
        return remote(GS.at[p, k, d, t], GR.at[p, k, d, t], gs.at[p, k, d, t], gr.at[p, k, d, t], nbr[d])

    def halves(v, q):
        return v[q * 64 : (q + 1) * 64, :]

    def scatter_first(p, k):
        hh = 1 - h if k == 0 else h
        g = grad_block(p, at_x(2), hh)
        for d in range(2):
            GS[p, k, d, 0] = halves(g, d).astype(BF)
            send(g_x(p, k, d, 0))
        for d in range(2):
            g = grad_block(p, at_x(step[d]), hh)
            GS[p, k, d, 1] = halves(g, 1 - d).astype(BF)
            send(g_x(p, k, d, 1))
            GK[p, k, d] = halves(g, d)
        g = grad_block(p, x, hh)
        for q in range(2):
            GK[p, k, 2 + q] = halves(g, q)

    def scatter_second(p, k):
        for d in range(2):
            g_x(p, k, d, 0).wait_recv()
            GS[p, k, d, 2] = (GK[p, k, d] + GR[p, k, d, 0].astype(F32)).astype(BF)
            send(g_x(p, k, d, 2))

    def scatter_sum(p, k, q):
        return GK[p, k, 2 + q] + GR[p, k, 1 - q, 1].astype(F32) + GR[p, k, q, 2].astype(F32)

    def scatter_got(p, k):
        for d in range(2):
            g_x(p, k, d, 1).wait_recv()
        for d in range(2):
            g_x(p, k, d, 2).wait_recv()

    g_y = [remote(YS.at[p], YR.at[p], gys.at[p], gyr.at[p], anti) for p in range(2)]

    def cross(p):
        scatter_got(p, 0)
        for q in range(2):
            YS[p, pl.ds(q * 64, 64), :] = scatter_sum(p, 0, q).astype(BF)
        send(g_y[p])

    def finish(p):
        scatter_got(p, 1)
        g_y[p].wait_recv()
        total = jnp.concatenate(
            [scatter_sum(p, 1, q) + YR[p, pl.ds(q * 64, 64), :].astype(F32) for q in range(2)], axis=0
        )
        wg_o[:, pl.ds(p * HALF, HALF)] = total.T * INV

    partial[0].wait_recv()
    activation_out(0)
    gradient(0)
    neighbours(1, 1)
    far(1, 1)
    send(partial[1])
    scatter_first(0, 0)
    z_round(4)
    activation_z(0)
    partial[1].wait_recv()
    activation_out(1)
    gradient(1)
    scatter_second(0, 0)
    scatter_first(1, 0)
    activation_z(1)
    scatter_first(0, 1)
    cross(0)
    scatter_second(1, 0)
    scatter_first(1, 1)
    scatter_second(0, 1)
    cross(1)
    scatter_second(1, 1)
    finish(0)
    activation_end(0)
    finish(1)
    activation_end(1)

    for cp in sent:
        cp.wait_send()

    for p in range(2):
        act_z_all(p).wait_send()


def hand_over(act, wg, act_o, wg_o, act_v, wg_v, sem):
    into = [
        pltpu.make_async_copy(wg, wg_v, sem.at[0]),
        pltpu.make_async_copy(act, act_v, sem.at[1]),
    ]
    out = [
        pltpu.make_async_copy(wg_v, wg_o, sem.at[2]),
        pltpu.make_async_copy(act_v, act_o, sem.at[3]),
    ]
    for cp in into:
        cp.start()
    for arrived, cp in zip(into, out):
        arrived.wait()
        cp.start()
    for cp in out:
        cp.wait()


def per_device(tokens, cotangent, codes, scales):
    dma = pltpu.SemaphoreType.DMA
    hbm = pl.BlockSpec(memory_space=pltpu.HBM)
    vmem = pl.BlockSpec(memory_space=pltpu.VMEM)
    out_shape = (
        jax.ShapeDtypeStruct((OWN, NZ * NYL * COLS), BF),
        jax.ShapeDtypeStruct((ROWS, COLS), F32),
    )
    act, wg = pl.pallas_call(
        body,
        out_shape=out_shape,
        in_specs=[hbm, hbm, hbm, hbm],
        out_specs=(vmem, vmem),
        scratch_shapes=[
            pltpu.VMEM((2, BLOCKS, TOK, ROWS), BF),
            pltpu.VMEM((2, TOK, COLS), BF),
            pltpu.VMEM((ROWS, COLS), BF),
            pltpu.VMEM((2, COLS), BF),
            pltpu.VMEM((BLOCKS, 2, ROWS, HALF), BF),
            pltpu.VMEM((2, 2, TOK, HALF), F32),
            pltpu.VMEM((2, 2, TOK, HALF), F32),
            pltpu.VMEM((2, 2, HALF, TOK), BF),
            pltpu.VMEM((2, TOK + 8, HALF), F32),
            pltpu.VMEM((2, NYL, NZ, 8, HALF), BF),
            pltpu.VMEM((2, NYL, NZ, 8, HALF), BF),
            pltpu.VMEM((2, NZ, NYL, 8, HALF), BF),
            pltpu.VMEM((2, 2, 4, 64, ROWS), F32),
            pltpu.VMEM((2, 2, 2, 3, 64, ROWS), BF),
            pltpu.VMEM((2, 2, 2, 3, 64, ROWS), BF),
            pltpu.VMEM((2, HALF, ROWS), BF),
            pltpu.VMEM((2, HALF, ROWS), BF),
            dma((3 + BLOCKS,)),
            dma((9,)), dma((9,)),
            dma((2, 2)), dma((2, 2)),
            dma((2, 2, 2, 3)), dma((2, 2, 2, 3)),
            dma((2,)), dma((2,)),
            dma((2, 2, 2, 3)), dma((2, 2, 2, 3)),
            dma((2,)), dma((2,)),
            dma((2, NYL)), dma((2, NYL)),
            dma((2,)), dma((2,)),
            pltpu.SemaphoreType.REGULAR((4,)),
        ],
        compiler_params=pltpu.CompilerParams(
            collective_id=0, has_side_effects=True, vmem_limit_bytes=61 << 20
        ),
        name="panel",
    )(tokens, cotangent, codes, scales)
    return pl.pallas_call(
        hand_over,
        out_shape=out_shape,
        in_specs=[hbm, hbm],
        out_specs=(hbm, hbm),
        scratch_shapes=[
            pltpu.VMEM((OWN, NZ * NYL * COLS), BF),
            pltpu.VMEM((ROWS, COLS), F32),
            dma((4,)),
        ],
        compiler_params=pltpu.CompilerParams(vmem_limit_bytes=61 << 20),
        name="hand_over",
    )(act, wg)


def solution(mesh):
    return jax.shard_map(
        per_device,
        mesh=mesh,
        in_specs=(P("rep", None), P("rep", "fsdp"), P("rep", "fsdp"), P("rep", "fsdp")),
        out_specs=(P(("rep", "fsdp"), None), P("rep", "fsdp")),
        check_vma=False,
    )
```
